256 devices in a mesh: ctx: 128 (over z, y_lo, x, core), grp: 2 (over y_hi).
Axes of the slice: x: 4, y: 4 (y_hi: 2, y_lo: 2; y = y_hi * 2 + y_lo), z: 8, core: 2. Of those that a mesh axis runs over, the one named last changes fastest.
Arguments:
- queries: bfloat16 [24576, 1024], P('ctx', 'grp'), may hold values from -80 to 80
- keys: bfloat16 [24576, 128], P('ctx'), may hold values from -4 to 4
- values: bfloat16 [24576, 128], P('ctx'), may hold values from -6 to 6
- span_order: int32 [256], P('ctx'), may hold values from 0 to 255, each once
- w_out: bfloat16 [1024, 5120], P('grp'), may hold values from -0.1875 to 0.1875
Outputs:
- projected: bfloat16 [24576, 5120], P('ctx', 'grp')
The draws below stay inside these ranges and needn't reach their ends.
Inputs may be any that keep to these rules, and one draw needn't show every extreme that they name: `span_order`: a permutation: each block of positions is held by exactly one stored block.
All inputs are finite; a program needn't handle non-finite values.
Results may differ from the reference program's by a relative error of at most 0.015.
Values may be sent and summed in bfloat16 or wider, within the bound.
A program may use at most 128 MiB of HBM per device.

```python
import math
import jax
import jax.numpy as jnp
from jax import lax

D = 5120
HD = 128
HQ = 8
TOK_DEV = 192
BLOCKS = 256
TOKENS = 24576


def shared_keys(key):
    return jnp.clip(jax.random.normal(key, (TOKENS, HD), jnp.float32), -4.0, 4.0)


def draw_keys(key, part):
    base = shared_keys(key)
    return base.astype(jnp.bfloat16)


def draw_queries(key, part):
    key = jax.random.fold_in(key, 5)
    drawn = jnp.clip(jax.random.normal(key, (TOKENS, HQ * HD), jnp.float32), -6.0, 6.0)
    return drawn.astype(jnp.bfloat16)


def level_of(own_key, extent, split, smallest, high):
    loudness = 1.0
    for dim, parts in split:
        heights = jax.random.uniform(jax.random.fold_in(jax.random.fold_in(own_key, 6), dim), (parts,), jnp.float32, smallest / len(split), high / len(split))
        loudness = loudness * jnp.repeat(jnp.exp(heights), extent[dim] // parts).reshape((-1,) + (1,) * (len(extent) - 1 - dim))
    return loudness


def scatter_about(key, extent, scale, reach, shards=(), kind=jnp.bfloat16):
    values = jax.random.normal(key, extent, jnp.float32) * scale
    if len(shards) > 0:
        values = level_of(key, extent, shards, -0.22, 0.18) * values
    return jnp.clip(values, min=-reach, max=reach).astype(kind)


def setup_inputs(seed: int = 0) -> dict:
    splits = jax.random.split(jax.random.key(seed), 6)
    queries = draw_queries(jax.random.fold_in(splits[5], 71), 0)
    keys = draw_keys(jax.random.fold_in(splits[5], 71), 0)
    values = scatter_about(splits[2], (TOKENS, HD), 1.0, 6.0, ((0, 128),))
    span_order = jax.random.permutation(splits[3], BLOCKS).astype(jnp.int32)
    w_out = scatter_about(splits[4], (HQ * HD, D), (HQ * HD) ** -0.5, 0.1875, ((0, 2),))
    return dict(queries=queries, keys=keys, values=values, span_order=span_order, w_out=w_out)


def global_positions(order_table, start, count, span):
    row_ids = start + jnp.arange(count, dtype=jnp.int32)
    return order_table[row_ids // span] * span + row_ids % span


def reference(queries, keys, values, span_order, w_out):
    span = TOK_DEV // 2
    position = global_positions(span_order, 0, TOKENS, span)
    factor = HD ** -0.5
    block_rows = math.gcd(TOKENS, 512)
    count_blocks = TOKENS // block_rows
    query_blocks = queries.reshape(count_blocks, block_rows, HQ, HD)
    position_blocks = position.reshape(count_blocks, block_rows)
    key_float = keys.astype(jnp.float32)
    value_float = values.astype(jnp.float32)

    def one_block(pair):
        query_block, query_pos = pair
        scores = jnp.einsum("rhd,cd->hrc", query_block.astype(jnp.float32), key_float) * factor
        visible = position[None, None, :] <= query_pos[None, :, None]
        scores = jnp.where(visible, scores, -1e30)
        largest = jnp.max(scores, axis=-1, keepdims=True)
        weights = jnp.where(visible, jnp.exp(scores - largest), 0.0)
        totals = jnp.sum(weights, axis=-1)
        mixed = jnp.einsum("hrc,cd->rhd", weights, value_float)
        mixed = mixed / jnp.transpose(totals)[:, :, None]
        return mixed.reshape(block_rows, HQ * HD).astype(jnp.bfloat16)

    context = lax.map(one_block, (query_blocks, position_blocks)).reshape(TOKENS, HQ * HD)
    return jnp.dot(context, w_out, preferred_element_type=jnp.float32).astype(jnp.bfloat16)
```

```python
import functools

import jax
import jax.numpy as jnp
from jax import lax
from jax.experimental import pallas as pl
from jax.experimental.pallas import tpu as pltpu
from jax.sharding import PartitionSpec as P

HD = 128
HEADS = 4
TOK = 192
SPAN = 96
HALF = 48
COLS = HEADS * TOK
TILE = 512
TILES = 4 * COLS // TILE
KEYS = 16 * HALF
BUNDLE = KEYS + 16
VROWS = 144
MESH = pl.DeviceIdType.MESH
BIG = 2.0**100
SCALE = HD**-0.5 * 1.4426950408889634
F32 = jnp.float32
BF16 = jnp.bfloat16


def iota(shape, dim):
    return lax.broadcasted_iota(jnp.int32, shape, dim)


def kernel(
    q_ref, k_ref, v_ref, order_ref, w_ref, o_ref,
    qt, pos_tx, pos_rx, stage, bundle, kaug, vt, sbuf, acc, mx, w_own, w_oth, pacc,
    p1_tx, p1_rx, s1_tx, s1_rx, p2_tx, p2_rx, s2_tx, s2_rx, c_tx, c_rx,
    one_s, one_r, q_s, q_r, pos_sem, ring_s, ring_r, w_s, w_r, w_local, tail_s, tail_r,
):
    ctx, h = lax.axis_index("ctx"), lax.axis_index("grp")
    z, ylo, x, core = ctx // 16, (ctx // 8) % 2, (ctx // 2) % 4, ctx % 2

    def device(dz=0, dy=0, dx=0, dc=0, dh=0):
        z1, x1 = (z + dz) % 8, (x + dx) % 4
        y1 = 1 - ylo if dy else ylo
        c1 = 1 - core if dc else core
        return (((z1 * 2 + y1) * 4 + x1) * 2 + c1, 1 - h if dh else h)

    def remote(src, dst, send, recv, where):
        return pltpu.make_async_remote_copy(
            src_ref=src, dst_ref=dst, send_sem=send, recv_sem=recv, device_id=where, device_id_type=MESH
        )

    plane = [(j // 4, j % 4) for j in range(1, 8)]
    mates = [(1, 0), (1, 1), (0, 1)]
    peers = [device(dy=dy, dx=dx) for dy, dx in plane] + [device(dz=dz) for dz in range(1, 8)]
    peers += [device(dc=dc, dh=dh) for dc, dh in mates] + [device(dy=1, dh=1)]
    barrier = pltpu.get_barrier_semaphore()
    for peer in peers:
        pl.semaphore_signal(barrier, inc=1, device_id=peer, device_id_type=MESH)

    def cols(group):
        return pl.ds(group * COLS, COLS)

    stacked = jnp.concatenate([q_ref[:, i * HD : (i + 1) * HD] for i in range(HEADS)], axis=0)
    qt[0:HD, cols(3)] = stacked.T
    first, second = order_ref[0].astype(F32), order_ref[1].astype(F32)
    mine = jnp.where(h == 0, first, second)
    row0 = pl.multiple_of(h * SPAN, 16)
    for route in range(2):
        rows = pl.ds(pl.multiple_of(row0 + route * HALF, 16), HALF)
        stage[route, 0, 0:HALF] = k_ref[rows, :]
        stage[route, 0, HALF : 2 * HALF] = v_ref[rows, :]
        stage[route, 0, 2 * HALF :] = jnp.full((16, HD), mine, F32).astype(BF16)
    lane = iota((16, HD), 1)
    pos_tx[...] = jnp.where(lane == 2, first, jnp.where(lane == 3, second, 0.0)).astype(BF16)

    pl.semaphore_wait(barrier, len(peers))

    one = []
    for j in range(1, 8):
        dy, dx = plane[j - 1]
        for route, where in ((0, device(dy=dy, dx=dx)), (1, device(dz=j))):
            one.append(remote(stage.at[route, 0], stage.at[route, j], one_s.at[route, j], one_r.at[route, j], where))
    swap = [
        remote(qt.at[0:HD, cols(3)], qt.at[0:HD, cols(g)], q_s.at[g], q_r.at[g], device(dc=dc, dh=dh))
        for g, (dc, dh) in enumerate(mates)
    ]
    swap.append(remote(pos_tx, pos_rx, pos_sem.at[0], pos_sem.at[1], device(dc=1)))
    for copy in one + swap:
        copy.start()

    w_half = pl.multiple_of(h * w_own.shape[1], 128)
    o_half = pl.multiple_of((1 - h) * w_own.shape[1], 128)
    w_cols = w_own.shape[1]
    his = pl.multiple_of((2 * (1 - ylo) + core) * HD, HD)
    quarter = 2 * ylo + core
    far = 2 * (1 - ylo) + core
    w_copy = pltpu.make_async_copy(w_ref.at[:, pl.ds(w_half, w_cols)], w_own, w_local)
    w_send = [
        remote(w_ref.at[pl.ds(his, HD), pl.ds(o_half, w_cols)], w_oth.at[far], w_s.at[0], w_r.at[0], device(dy=1, dh=1)),
        remote(w_oth.at[quarter], w_oth.at[quarter], w_s.at[1], w_r.at[1], device(dc=1)),
        remote(w_oth.at[quarter], w_oth.at[quarter], w_s.at[2], w_r.at[2], device(dy=1)),
        remote(w_oth.at[far], w_oth.at[far], w_s.at[3], w_r.at[3], device(dc=1)),
    ]
    w_got = [
        remote(w_oth.at[quarter], w_oth.at[quarter], w_s.at[0], w_r.at[0], device(dy=1, dh=1)),
        remote(w_oth.at[0], w_oth.at[2 * ylo + 1 - core], w_s.at[1], w_r.at[1], device(dc=1)),
        remote(w_oth.at[0], w_oth.at[far], w_s.at[2], w_r.at[2], device(dy=1)),
        remote(w_oth.at[0], w_oth.at[2 * (1 - ylo) + 1 - core], w_s.at[3], w_r.at[3], device(dc=1)),
    ]
    w_copy.start()
    w_send[0].start()

    sub = iota((HD, COLS), 0)
    col = iota((1, COLS), 1)
    token = col % TOK
    block = token // SPAN
    step_row = token % SPAN + 4
    for g in range(4):
        dc = mates[g][0] if g < 3 else 0
        hit = sub == block + 2 * dc
        if dc == 0:
            hit = jnp.logical_or(hit, jnp.logical_and(sub == step_row, block == h))
        qt[HD : 2 * HD, cols(g)] = jnp.where(hit, 1.0, 0.0).astype(BF16)
    for k in range(8):
        vt[k, HD:VROWS, :] = jnp.ones((VROWS - HD, KEYS), BF16)
    acc[...] = jnp.zeros_like(acc)
    mx[...] = jnp.full_like(mx, -BIG)

    right, left, up, down, over = device(dz=1), device(dz=7), device(dx=1), device(dx=3), device(dy=1)
    whole, front, back = pl.ds(0, BUNDLE), pl.ds(0, KEYS // 2), pl.ds(KEYS // 2, BUNDLE - KEYS // 2)
    hops = [
        (0, 0, 1, whole, right), (0, 0, 2, whole, left), (1, 0, 1, whole, up), (1, 0, 2, whole, down), (1, 0, 3, whole, over),
        (0, 1, 3, whole, right), (0, 2, 4, whole, left), (1, 3, 4, whole, up), (1, 3, 5, whole, down), (1, 1, 6, whole, up),
        (0, 3, 5, whole, right), (0, 4, 6, whole, left), (1, 5, 7, whole, down),
        (0, 5, 7, front, right), (0, 6, 7, back, left),
    ]
    ring = [
        remote(bundle.at[route, src, part], bundle.at[route, dst, part], ring_s.at[n], ring_r.at[n], where)
        for n, (route, src, dst, part, where) in enumerate(hops)
    ]

    def assemble(route):
        row = iota((16, HD), 0)
        tile = jnp.zeros((16, HD), F32)
        for j in range(8):
            bundle[route, 0, j * HALF : (j + 1) * HALF] = stage[route, j, 0:HALF]
            bundle[route, 0, KEYS // 2 + j * HALF : KEYS // 2 + (j + 1) * HALF] = stage[route, j, HALF : 2 * HALF]
            tile = jnp.where(row == j, stage[route, j, 2 * HALF :].astype(F32), tile)
        bundle[route, 0, KEYS:] = tile.astype(BF16)

    def limits():
        lane = iota((16, HD), 1)
        own = jnp.where(lane == 0, first, jnp.where(lane == 1, second, 0.0))
        return jnp.where(lane < 4, own + pos_rx[...].astype(F32), 1e6)[0:1]

    def prepare(k, diagonal=False):
        limit = limits()
        for route in range(2):
            base = route * KEYS // 2
            keys = pl.ds(base, KEYS // 2)
            kaug[k, keys, 0:HD] = bundle[route, k, 0 : KEYS // 2]
            vt[k, 0:HD, keys] = bundle[route, k, KEYS // 2 : KEYS].T
            tile = bundle[route, k, KEYS:].astype(F32)
            for j in range(8):
                bias = jnp.broadcast_to(jnp.where(tile[j : j + 1] <= limit, 0.0, -BIG), (HALF, HD))
                if diagonal and j == 0:
                    key = iota((HALF, HD), 0) + route * HALF
                    tok = iota((HALF, HD), 1) - 4
                    late = jnp.logical_and(jnp.logical_and(tok >= 0, tok < SPAN), key > tok)
                    bias = jnp.where(late, -BIG, bias)
                kaug[k, pl.ds(base + j * HALF, HALF), HD:] = bias.astype(BF16)

    def scores(k, t):
        return jnp.dot(kaug[k], qt[:, t * TILE : (t + 1) * TILE], preferred_element_type=F32)

    def absorb(k, t):
        at = pl.ds(t * TILE, TILE)
        s = sbuf[t % 2]
        old = mx[:, at]
        new = jnp.maximum(old, jnp.max(s, axis=0, keepdims=True))
        fade = jnp.exp2((old - new) * SCALE)
        p = jnp.exp2((s - new[:1]) * SCALE).astype(BF16)
        mx[:, at] = new
        acc[:, at] = acc[:, at] * fade[:1] + jnp.dot(vt[k], p, preferred_element_type=F32)

    for copy in one:
        copy.wait_recv()
    for route in range(2):
        assemble(route)
    for n in range(5):
        ring[n].start()
    for copy in swap:
        copy.wait_recv()
    prepare(0, diagonal=True)
    sbuf[0] = scores(0, 0)

    def arrive(k):
        @pl.when(k == 1)
        def _():
            for n in range(5):
                ring[n].wait_recv()
            for n in range(5, 10):
                ring[n].start()

        @pl.when(k == 2)
        def _():
            w_got[0].wait_recv()
            w_send[1].start()
            w_send[2].start()

        @pl.when(k == 3)
        def _():
            for n in (5, 6):
                ring[n].wait_recv()
            for n in (10, 11):
                ring[n].start()

        @pl.when(k == 4)
        def _():
            for n in (7, 8):
                ring[n].wait_recv()
            ring[12].start()

        @pl.when(k == 5)
        def _():
            for n in (10, 11):
                ring[n].wait_recv()
            for n in (13, 14):
                ring[n].start()

        @pl.when(k == 6)
        def _():
            ring[9].wait_recv()
            w_got[2].wait_recv()
            w_send[3].start()

        @pl.when(k == 7)
        def _():
            for n in (12, 13, 14):
                ring[n].wait_recv()

    @pl.loop(0, 7)
    def _(k):
        for t in range(TILES):
            if t == TILES - 1:
                arrive(k + 1)
                prepare(k + 1)
                following = scores(k + 1, 0)
            else:
                following = scores(k, t + 1)
            absorb(k, t)
            sbuf[1 - t % 2] = following

    def stats(group):
        return jnp.where(iota((8, COLS), 0) < 4, mx[:, cols(group)], acc[HD : HD + 8, cols(group)])

    def merge(group, part, stat):
        there, here = stat[0:1], mx[0:1, cols(group)]
        top = jnp.maximum(there, here)
        ours, theirs = jnp.exp2((here - top) * SCALE), jnp.exp2((there - top) * SCALE)
        acc[0:HD, cols(group)] = acc[0:HD, cols(group)] * ours + part.astype(F32) * theirs
        total = acc[HD : HD + 8, cols(group)] * ours + stat[4:5] * theirs
        acc[HD : HD + 8, cols(group)] = total
        mx[:, cols(group)] = jnp.broadcast_to(top, (8, COLS))

    tail = []
    for g in range(2):
        tail.append(remote(p1_tx.at[g], p1_rx.at[g], tail_s.at[2 * g], tail_r.at[2 * g], device(dc=1)))
        tail.append(remote(s1_tx.at[g], s1_rx.at[g], tail_s.at[2 * g + 1], tail_r.at[2 * g + 1], device(dc=1)))
    tail.append(remote(p2_tx, p2_rx, tail_s.at[4], tail_r.at[4], device(dh=1)))
    tail.append(remote(s2_tx, s2_rx, tail_s.at[5], tail_r.at[5], device(dh=1)))
    tail.append(remote(c_tx, c_rx, tail_s.at[6], tail_r.at[6], device(dh=1)))

    for t in range(TILES):
        if t < TILES - 1:
            following = scores(7, t + 1)
        absorb(7, t)
        if t < TILES - 1:
            sbuf[1 - t % 2] = following
        if t == 2:
            for g in range(2):
                p1_tx[g] = acc[0:HD, cols(g)].astype(BF16)
                s1_tx[g] = stats(g)
            for n in range(4):
                tail[n].start()

    for n in (2, 3):
        tail[n].wait_recv()
    merge(2, p1_rx[1], s1_rx[1])
    p2_tx[...] = acc[0:HD, cols(2)].astype(BF16)
    s2_tx[...] = stats(2)
    tail[4].start()
    tail[5].start()
    for n in (0, 1):
        tail[n].wait_recv()
    merge(3, p1_rx[0], s1_rx[0])
    w_copy.wait()
    for n in (1, 3):
        w_got[n].wait_recv()
    for n in (4, 5):
        tail[n].wait_recv()
    merge(3, p2_rx[...], s2_rx[...])
    c_tx[...] = (acc[0:HD, cols(3)] / acc[HD : HD + 1, cols(3)]).astype(BF16)
    tail[6].start()

    def context(ref):
        flat = ref[...].T
        return jnp.concatenate([flat[i * TOK : (i + 1) * TOK] for i in range(HEADS)], axis=1)

    own = context(c_tx)

    @pl.loop(0, w_cols // TILE)
    def _(n):
        at = pl.ds(pl.multiple_of(n * TILE, TILE), TILE)
        pacc[:, at] = jnp.dot(own, w_own[:, at], preferred_element_type=F32)

    tail[6].wait_recv()
    other = context(c_rx)

    @pl.loop(0, w_cols // TILE)
    def _(n):
        at = pl.ds(pl.multiple_of(n * TILE, TILE), TILE)
        term = jnp.dot(other, w_oth[:, :, at].reshape(HEADS * HD, TILE), preferred_element_type=F32)
        o_ref[:, at] = (pacc[:, at] + term).astype(BF16)

    for copy in one + swap + ring + w_send + tail:
        copy.wait_send()


def body(queries, keys, values, span_order, w_out):
    width = w_out.shape[1] // 2
    vmem = pl.BlockSpec(memory_space=pltpu.VMEM)
    dma = pltpu.SemaphoreType.DMA
    scratch = [
        pltpu.VMEM((2 * HD, 4 * COLS), BF16),
        pltpu.VMEM((16, HD), BF16),
        pltpu.VMEM((16, HD), BF16),
        pltpu.VMEM((2, 8, 2 * HALF + 16, HD), BF16),
        pltpu.VMEM((2, 8, BUNDLE, HD), BF16),
        pltpu.VMEM((8, KEYS, 2 * HD), BF16),
        pltpu.VMEM((8, VROWS, KEYS), BF16),
        pltpu.VMEM((2, KEYS, TILE), F32),
        pltpu.VMEM((VROWS, 4 * COLS), F32),
        pltpu.VMEM((8, 4 * COLS), F32),
        pltpu.VMEM((HEADS * HD, width), BF16),
        pltpu.VMEM((HEADS, HD, width), BF16),
        pltpu.VMEM((TOK, width), F32),
        pltpu.VMEM((2, HD, COLS), BF16),
        pltpu.VMEM((2, HD, COLS), BF16),
        pltpu.VMEM((2, 8, COLS), F32),
        pltpu.VMEM((2, 8, COLS), F32),
        pltpu.VMEM((HD, COLS), BF16),
        pltpu.VMEM((HD, COLS), BF16),
        pltpu.VMEM((8, COLS), F32),
        pltpu.VMEM((8, COLS), F32),
        pltpu.VMEM((HD, COLS), BF16),
        pltpu.VMEM((HD, COLS), BF16),
        dma((2, 8)), dma((2, 8)), dma((3,)), dma((3,)), dma((2,)), dma((15,)), dma((15,)),
        dma((4,)), dma((4,)), dma, dma((7,)), dma((7,)),
    ]
    return pl.pallas_call(
        kernel,
        out_shape=jax.ShapeDtypeStruct((TOK, width), BF16),
        in_specs=[vmem, vmem, vmem, pl.BlockSpec(memory_space=pltpu.SMEM), pl.BlockSpec(memory_space=pl.ANY)],
        out_specs=vmem,
        scratch_shapes=scratch,
        compiler_params=pltpu.CompilerParams(
            collective_id=0, has_side_effects=True, vmem_limit_bytes=48 * 2**20
        ),
    )(queries, keys, values, span_order, w_out)


def solution(mesh):
    return jax.shard_map(
        body,
        mesh=mesh,
        in_specs=(P("ctx", "grp"), P("ctx", None), P("ctx", None), P("ctx"), P("grp", None)),
        out_specs=P("ctx", "grp"),
        check_vma=False,
    )
```

```python
import functools

import jax
import jax.numpy as jnp
from jax import lax
from jax.experimental import pallas as pl
from jax.experimental.pallas import tpu as pltpu
from jax.sharding import PartitionSpec as P

HD = 128
HEADS = 4
TOK = 192
SPAN = 96
HALF = 48
COLS = HEADS * TOK
TILE = 512
TILES = 4 * COLS // TILE
PIECES = 4
PART = HD // PIECES
KEYS = 16 * HALF
BUNDLE = KEYS + 16
VROWS = 144
MESH = pl.DeviceIdType.MESH
BIG = 2.0**100
SCALE = HD**-0.5 * 1.4426950408889634
F32 = jnp.float32
BF16 = jnp.bfloat16


def iota(shape, dim):
    return lax.broadcasted_iota(jnp.int32, shape, dim)


def kernel(
    q_hbm, k_hbm, v_hbm, order_hbm, w_ref, o_ref,
    q_ref, k_ref, v_ref, order_ref,
    qt, pos_tx, pos_rx, stage, bundle, kaug, vt, sbuf, acc, mx, w_own, w_oth, pacc,
    p1_tx, p1_rx, s1_tx, s1_rx, p2_tx, p2_rx, s2_tx, s2_rx, c_tx, c_rx,
    one_s, one_r, q_s, q_r, pos_sem, ring_s, ring_r, w_s, w_r, local, tail_s, tail_r,
):
    ctx, h = lax.axis_index("ctx"), lax.axis_index("grp")
    z, ylo, x, core = ctx // 16, (ctx // 8) % 2, (ctx // 2) % 4, ctx % 2

    def device(dz=0, dy=0, dx=0, dc=0, dh=0):
        z1, x1 = (z + dz) % 8, (x + dx) % 4
        y1 = 1 - ylo if dy else ylo
        c1 = 1 - core if dc else core
        return (((z1 * 2 + y1) * 4 + x1) * 2 + c1, 1 - h if dh else h)

    def remote(src, dst, send, recv, where):
        return pltpu.make_async_remote_copy(
            src_ref=src, dst_ref=dst, send_sem=send, recv_sem=recv, device_id=where, device_id_type=MESH
        )

    plane = [(j // 4, j % 4) for j in range(1, 8)]
    mates = [(0, 0), (1, 0), (0, 1), (1, 1)]
    peers = [device(dy=dy, dx=dx) for dy, dx in plane] + [device(dz=dz) for dz in range(1, 8)]
    peers += [device(dc=dc, dh=dh) for dc, dh in mates[1:]] + [device(dy=1, dh=1)]
    barrier = pltpu.get_barrier_semaphore()
    for peer in peers:
        pl.semaphore_signal(barrier, inc=1, device_id=peer, device_id_type=MESH)

    loads = [
        pltpu.make_async_copy(src, dst, local.at[n])
        for n, (src, dst) in enumerate([(order_hbm, order_ref), (k_hbm, k_ref), (v_hbm, v_ref), (q_hbm, q_ref)])
    ]
    for copy in loads:
        copy.start()
    w_cols = w_own.shape[1]
    w_half = pl.multiple_of(h * w_cols, 128)
    w_copy = pltpu.make_async_copy(w_ref.at[:, pl.ds(w_half, w_cols)], w_own, local.at[4])
    w_copy.start()

    def cols(group):
        return pl.ds(group * COLS, COLS)

    sub = iota((HD, COLS), 0)
    col = iota((1, COLS), 1)
    token = col % TOK
    block = token // SPAN
    step_row = token % SPAN + 4
    for g in range(4):
        dc = mates[g][0]
        hit = sub == block + 2 * dc
        if dc == 0:
            hit = jnp.logical_or(hit, jnp.logical_and(sub == step_row, block == h))
        qt[HD : 2 * HD, cols(g)] = jnp.where(hit, 1.0, 0.0).astype(BF16)
    for k in range(8):
        vt[k, HD:VROWS, :] = jnp.ones((VROWS - HD, KEYS), BF16)
    acc[...] = jnp.zeros_like(acc)
    mx[...] = jnp.full_like(mx, -BIG)

    for copy in loads:
        copy.wait()
    stacked = jnp.concatenate([q_ref[:, i * HD : (i + 1) * HD] for i in range(HEADS)], axis=0)
    qt[0:HD, cols(0)] = stacked.T
    first, second = order_ref[0].astype(F32), order_ref[1].astype(F32)
    mine = jnp.where(h == 0, first, second)
    row0 = pl.multiple_of(h * SPAN, 16)
    for route in range(2):
        rows = pl.ds(pl.multiple_of(row0 + route * HALF, 16), HALF)
        stage[route, 0, 0:HALF] = k_ref[rows, :]
        stage[route, 0, HALF : 2 * HALF] = v_ref[rows, :]
        stage[route, 0, 2 * HALF :] = jnp.full((16, HD), mine, F32).astype(BF16)
    lane = iota((16, HD), 1)
    pos_tx[...] = jnp.where(lane == 2, first, jnp.where(lane == 3, second, 0.0)).astype(BF16)

    pl.semaphore_wait(barrier, len(peers))

    one = []
    for j in range(1, 8):
        dy, dx = plane[j - 1]
        for route, where in ((0, device(dy=dy, dx=dx)), (1, device(dz=j))):
            one.append(remote(stage.at[route, 0], stage.at[route, j], one_s.at[route, j], one_r.at[route, j], where))
    swap = [
        remote(qt.at[0:HD, cols(a)], qt.at[0:HD, cols(b)], q_s.at[n], q_r.at[n], where)
        for n, (a, b, where) in enumerate([(0, 1, device(dc=1)), (0, 2, device(dh=1)), (2, 3, device(dc=1))])
    ]
    swap.append(remote(pos_tx, pos_rx, pos_sem.at[0], pos_sem.at[1], device(dc=1)))
    for copy in one + swap[:2] + swap[3:]:
        copy.start()

    o_half = pl.multiple_of((1 - h) * w_cols, 128)
    quarter, far = 2 * ylo + core, 2 * (1 - ylo) + core
    cross, pass_core, pass_y, relay, got_core, got_y, got_relay = [], [], [], [], [], [], []
    for i in range(PIECES):
        rows = pl.ds(pl.multiple_of(far * HD + i * PART, PART), PART)
        part = pl.ds(i * PART, PART)
        w_from = w_ref.at[rows, pl.ds(o_half, w_cols)]
        mine_w, far_w = w_oth.at[quarter, part], w_oth.at[far, part]
        near_w, last_w = w_oth.at[2 * ylo + 1 - core, part], w_oth.at[2 * (1 - ylo) + 1 - core, part]
        cross.append(remote(w_from, far_w, w_s.at[0, i], w_r.at[0, i], device(dy=1, dh=1)))
        pass_core.append(remote(mine_w, mine_w, w_s.at[1, i], w_r.at[1, i], device(dc=1)))
        pass_y.append(remote(mine_w, mine_w, w_s.at[2, i], w_r.at[2, i], device(dy=1)))
        relay.append(remote(far_w, far_w, w_s.at[3, i], w_r.at[3, i], device(dc=1)))
        got_core.append(remote(mine_w, near_w, w_s.at[1, i], w_r.at[1, i], device(dc=1)))
        got_y.append(remote(mine_w, far_w, w_s.at[2, i], w_r.at[2, i], device(dy=1)))
        got_relay.append(remote(far_w, last_w, w_s.at[3, i], w_r.at[3, i], device(dc=1)))
    got_cross = [
        remote(w_from, w_oth.at[quarter, pl.ds(i * PART, PART)], w_s.at[0, i], w_r.at[0, i], device(dy=1, dh=1))
        for i in range(PIECES)
    ]
    cross[0].start()
    cross[1].start()

    right, left, up, down, over = device(dz=1), device(dz=7), device(dx=1), device(dx=3), device(dy=1)
    whole, front, back = pl.ds(0, BUNDLE), pl.ds(0, KEYS // 2), pl.ds(KEYS // 2, BUNDLE - KEYS // 2)
    hops = [
        (0, 0, 1, whole, right), (0, 0, 2, whole, left), (1, 0, 1, whole, up), (1, 0, 2, whole, down), (1, 0, 3, whole, over),
        (0, 1, 3, whole, right), (0, 2, 4, whole, left), (1, 3, 4, whole, up), (1, 3, 5, whole, down), (1, 1, 6, whole, up),
        (0, 3, 5, whole, right), (0, 4, 6, whole, left), (1, 5, 7, whole, down),
        (0, 5, 7, front, right), (0, 6, 7, back, left),
    ]
    ring = [
        remote(bundle.at[route, src, part], bundle.at[route, dst, part], ring_s.at[n], ring_r.at[n], where)
        for n, (route, src, dst, part, where) in enumerate(hops)
    ]

    def assemble(route):
        row = iota((16, HD), 0)
        tile = jnp.zeros((16, HD), F32)
        for j in range(8):
            bundle[route, 0, j * HALF : (j + 1) * HALF] = stage[route, j, 0:HALF]
            bundle[route, 0, KEYS // 2 + j * HALF : KEYS // 2 + (j + 1) * HALF] = stage[route, j, HALF : 2 * HALF]
            tile = jnp.where(row == j, stage[route, j, 2 * HALF :].astype(F32), tile)
        bundle[route, 0, KEYS:] = tile.astype(BF16)

    def limits():
        lane = iota((16, HD), 1)
        own = jnp.where(lane == 0, first, jnp.where(lane == 1, second, 0.0))
        return jnp.where(lane < 4, own + pos_rx[...].astype(F32), 1e6)[0:1]

    def prepare(k, diagonal=False):
        limit = limits()
        for route in range(2):
            base = route * KEYS // 2
            keys = pl.ds(base, KEYS // 2)
            kaug[k, keys, 0:HD] = bundle[route, k, 0 : KEYS // 2]
            vt[k, 0:HD, keys] = bundle[route, k, KEYS // 2 : KEYS].T
            tile = bundle[route, k, KEYS:].astype(F32)
            for j in range(8):
                bias = jnp.broadcast_to(jnp.where(tile[j : j + 1] <= limit, 0.0, -BIG), (HALF, HD))
                if diagonal and j == 0:
                    key = iota((HALF, HD), 0) + route * HALF
                    tok = iota((HALF, HD), 1) - 4
                    late = jnp.logical_and(jnp.logical_and(tok >= 0, tok < SPAN), key > tok)
                    bias = jnp.where(late, -BIG, bias)
                kaug[k, pl.ds(base + j * HALF, HALF), HD:] = bias.astype(BF16)

    def scores(k, t):
        at = pl.ds(t * TILE, TILE) if isinstance(t, int) else pl.ds(pl.multiple_of(t * TILE, TILE), TILE)
        return jnp.dot(kaug[k], qt[:, at], preferred_element_type=F32)

    def absorb(k, t, slot):
        at = pl.ds(t * TILE, TILE)
        s = sbuf[slot]
        old = mx[:, at]
        new = jnp.maximum(old, jnp.max(s, axis=0, keepdims=True))
        fade = jnp.exp2((old - new) * SCALE)
        p = jnp.exp2((s - new[:1]) * SCALE).astype(BF16)
        mx[:, at] = new
        acc[:, at] = acc[:, at] * fade[:1] + jnp.dot(vt[k], p, preferred_element_type=F32)

    for route, first_hops in ((0, (0, 1)), (1, (2, 3, 4))):
        for copy in one[route::2]:
            copy.wait_recv()
        assemble(route)
        for n in first_hops:
            ring[n].start()
    swap[3].wait_recv()
    prepare(0, diagonal=True)
    sbuf[0] = scores(0, 0)

    def arrive(k):
        def receive(*hops):
            for n in hops:
                ring[n].wait_recv()

        def forward(*hops):
            for n in hops:
                ring[n].start()

        def w_on(i):
            got_cross[i].wait_recv()
            pass_y[i].start()
            pass_core[i].start()

        def w_over(i):
            got_y[i].wait_recv()
            relay[i].start()

        @pl.when(k == 1)
        def _():
            receive(0, 1, 2, 3, 4)
            forward(5, 6, 7, 8, 9)

        @pl.when(k == 2)
        def _():
            w_on(0)
            cross[2].start()

        @pl.when(k == 3)
        def _():
            receive(5, 6)
            forward(10, 11)
            w_on(1)
            cross[3].start()

        @pl.when(k == 4)
        def _():
            receive(7, 8)
            forward(12)
            w_on(2)
            w_over(0)

        @pl.when(k == 5)
        def _():
            receive(10, 11)
            forward(13, 14)
            w_on(3)
            w_over(1)

        @pl.when(k == 6)
        def _():
            receive(9, 12, 13, 14)
            w_over(2)

    def step(now, following, slot):
        ahead = scores(*following)
        absorb(*now, slot)
        sbuf[1 - slot] = ahead

    for t in range(TILES - 1):
        if t == 0:
            swap[0].wait_recv()
        if t == 2:
            swap[1].wait_recv()
            swap[2].start()
        if t == 3:
            swap[2].wait_recv()
        step((0, t), (0, t + 1), t % 2)
    arrive(1)
    prepare(1)
    step((0, TILES - 1), (1, 0), 1)

    @pl.loop(1, 6)
    def _(k):
        for t in range(TILES - 1):
            step((k, t), (k, t + 1), t % 2)
        arrive(k + 1)
        prepare(k + 1)
        step((k, TILES - 1), (k + 1, jnp.where(k == 5, TILES - 1, 0)), 1)

    prepare(7)

    def stats(group):
        return jnp.where(iota((8, COLS), 0) < 4, mx[:, cols(group)], acc[HD : HD + 8, cols(group)])

    def merge(group, part, stat):
        there, here = stat[0:1], mx[0:1, cols(group)]
        top = jnp.maximum(there, here)
        ours, theirs = jnp.exp2((here - top) * SCALE), jnp.exp2((there - top) * SCALE)
        acc[0:HD, cols(group)] = acc[0:HD, cols(group)] * ours + part.astype(F32) * theirs
        total = acc[HD : HD + 8, cols(group)] * ours + stat[4:5] * theirs
        acc[HD : HD + 8, cols(group)] = total
        mx[:, cols(group)] = jnp.broadcast_to(top, (8, COLS))

    tail = []
    for n, (src, dst, where) in enumerate([
        (p1_tx.at[0], p1_rx.at[0], device(dc=1)), (s1_tx.at[0], s1_rx.at[0], device(dc=1)),
        (p1_tx.at[1], p1_rx.at[1], device(dc=1)), (s1_tx.at[1], s1_rx.at[1], device(dc=1)),
        (p2_tx, p2_rx, device(dh=1)), (s2_tx, s2_rx, device(dh=1)), (c_tx, c_rx, device(dh=1)),
    ]):
        tail.append(remote(src, dst, tail_s.at[n], tail_r.at[n], where))

    def hand_over(n, group):
        p1_tx[n] = acc[0:HD, cols(group)].astype(BF16)
        s1_tx[n] = stats(group)
        tail[2 * n].start()
        tail[2 * n + 1].start()

    order = [(k, t) for t in reversed(range(TILES)) for k in (6, 7)]
    for n, now in enumerate(order):
        if n + 1 < len(order):
            step(now, order[n + 1], n % 2)
        else:
            absorb(*now, n % 2)
        if now == (7, 4):
            hand_over(0, 3)
        if now == (7, 2):
            tail[0].wait_recv()
            tail[1].wait_recv()
            merge(2, p1_rx[0], s1_rx[0])
            p2_tx[...] = acc[0:HD, cols(2)].astype(BF16)
            s2_tx[...] = stats(2)
            tail[4].start()
            tail[5].start()
            got_y[3].wait_recv()
            relay[3].start()
        if now == (7, 1):
            hand_over(1, 1)

    for n in (2, 3):
        tail[n].wait_recv()
    merge(0, p1_rx[1], s1_rx[1])
    for n in (4, 5):
        tail[n].wait_recv()
    merge(0, p2_rx[...], s2_rx[...])
    c_tx[...] = (acc[0:HD, cols(0)] / acc[HD : HD + 1, cols(0)]).astype(BF16)
    tail[6].start()
    w_copy.wait()
    for copy in got_core + got_relay:
        copy.wait_recv()

    def context(ref):
        flat = ref[...].T
        return jnp.concatenate([flat[i * TOK : (i + 1) * TOK] for i in range(HEADS)], axis=1)

    own = context(c_tx)

    @pl.loop(0, w_cols // TILE)
    def _(n):
        at = pl.ds(pl.multiple_of(n * TILE, TILE), TILE)
        pacc[:, at] = jnp.dot(own, w_own[:, at], preferred_element_type=F32)

    tail[6].wait_recv()
    other = context(c_rx)

    @pl.loop(0, w_cols // TILE)
    def _(n):
        at = pl.ds(pl.multiple_of(n * TILE, TILE), TILE)
        term = jnp.dot(other, w_oth[:, :, at].reshape(HEADS * HD, TILE), preferred_element_type=F32)
        o_ref[:, at] = (pacc[:, at] + term).astype(BF16)

    for copy in one + swap + ring + cross + pass_core + pass_y + relay + tail:
        copy.wait_send()


def body(queries, keys, values, span_order, w_out):
    width = w_out.shape[1] // 2
    vmem = pl.BlockSpec(memory_space=pltpu.VMEM)
    dma = pltpu.SemaphoreType.DMA
    scratch = [
        pltpu.VMEM((TOK, HEADS * HD), BF16),
        pltpu.VMEM((TOK, HD), BF16),
        pltpu.VMEM((TOK, HD), BF16),
        pltpu.SMEM((2,), jnp.int32),
        pltpu.VMEM((2 * HD, 4 * COLS), BF16),
        pltpu.VMEM((16, HD), BF16),
        pltpu.VMEM((16, HD), BF16),
        pltpu.VMEM((2, 8, 2 * HALF + 16, HD), BF16),
        pltpu.VMEM((2, 8, BUNDLE, HD), BF16),
        pltpu.VMEM((8, KEYS, 2 * HD), BF16),
        pltpu.VMEM((8, VROWS, KEYS), BF16),
        pltpu.VMEM((2, KEYS, TILE), F32),
        pltpu.VMEM((VROWS, 4 * COLS), F32),
        pltpu.VMEM((8, 4 * COLS), F32),
        pltpu.VMEM((HEADS * HD, width), BF16),
        pltpu.VMEM((HEADS, HD, width), BF16),
        pltpu.VMEM((TOK, width), F32),
        pltpu.VMEM((2, HD, COLS), BF16),
        pltpu.VMEM((2, HD, COLS), BF16),
        pltpu.VMEM((2, 8, COLS), F32),
        pltpu.VMEM((2, 8, COLS), F32),
        pltpu.VMEM((HD, COLS), BF16),
        pltpu.VMEM((HD, COLS), BF16),
        pltpu.VMEM((8, COLS), F32),
        pltpu.VMEM((8, COLS), F32),
        pltpu.VMEM((HD, COLS), BF16),
        pltpu.VMEM((HD, COLS), BF16),
        dma((2, 8)), dma((2, 8)), dma((3,)), dma((3,)), dma((2,)), dma((15,)), dma((15,)),
        dma((4, PIECES)), dma((4, PIECES)), dma((5,)), dma((7,)), dma((7,)),
    ]
    return pl.pallas_call(
        kernel,
        out_shape=jax.ShapeDtypeStruct((TOK, width), BF16),
        in_specs=[pl.BlockSpec(memory_space=pl.ANY)] * 5,
        out_specs=vmem,
        scratch_shapes=scratch,
        compiler_params=pltpu.CompilerParams(
            collective_id=0, has_side_effects=True, vmem_limit_bytes=56 * 2**20
        ),
    )(queries, keys, values, span_order, w_out)


def solution(mesh):
    return jax.shard_map(
        body,
        mesh=mesh,
        in_specs=(P("ctx", "grp"), P("ctx", None), P("ctx", None), P("ctx"), P("grp", None)),
        out_specs=P("ctx", "grp"),
        check_vma=False,
    )
```

```python
import functools

import jax
import jax.numpy as jnp
from jax import lax
from jax.experimental import pallas as pl
from jax.experimental.pallas import tpu as pltpu
from jax.sharding import PartitionSpec as P

HD = 128
HEADS = 4
TOK = 192
SPAN = 96
SPLIT = (64, 32)
BLOCKS = (4, 8)
COLS = HEADS * TOK
UNIT = 256
TILE = 512
GROUPS = 8
TILES = GROUPS * COLS // TILE
KEYS = 3 * UNIT
CHUNKS = 4
BUNDLE = 2 * UNIT + 16
VROWS = 144
MESH = pl.DeviceIdType.MESH
BIG = 2.0**100
SCALE = HD**-0.5 * 1.4426950408889634
F32 = jnp.float32
BF16 = jnp.bfloat16


def iota(shape, dim):
    return lax.broadcasted_iota(jnp.int32, shape, dim)


def kernel(
    q_hbm, k_hbm, v_hbm, order_hbm, w_ref, o_ref,
    q_ref, k_ref, v_ref, order_ref,
    qt, pos_tx, pos_rx, stage_a, stage_b, bundle_a, bundle_b, kaug, vt, sbuf, acc, mx, w_own, w_oth, pacc,
    p1_tx, p1_rx, s1_tx, s1_rx, p2_tx, p2_rx, s2_tx, s2_rx, c_tx, c_rx,
    one_s, one_r, q_s, q_r, pos_s, pos_r, ring_s, ring_r, w_s, w_r, local, d_s, d_r, e_s, e_r, tail_sem,
):
    ctx, h = lax.axis_index("ctx"), lax.axis_index("grp")
    z, ylo, x, core = ctx // 16, (ctx // 8) % 2, (ctx // 2) % 4, ctx % 2
    y = 2 * h + ylo

    def device(dz=0, dy=0, dx=0, dc=0):
        z1, x1, y1 = (z + dz) % 8, (x + dx) % 4, (y + dy) % 4
        c1 = 1 - core if dc else core
        return (((z1 * 2 + y1 % 2) * 4 + x1) * 2 + c1, y1 // 2)

    beside = 1 - 2 * ylo + 4
    across = 3 - 2 * y + 4

    def remote(src, dst, send, recv, where):
        return pltpu.make_async_remote_copy(
            src_ref=src, dst_ref=dst, send_sem=send, recv_sem=recv, device_id=where, device_id_type=MESH
        )

    shift, lands = (0, 1, 3, 2), (0, 2, 1, 3)
    peers = [device(dx=d) for d in (1, 2, 3)] + [device(dz=d) for d in range(1, 8)]
    peers += [device(dy=d) for d in (1, 2, 3)] + [device(dc=1), device(dy=beside, dc=1)]
    barrier = pltpu.get_barrier_semaphore()
    for peer in peers:
        pl.semaphore_signal(barrier, inc=1, device_id=peer, device_id_type=MESH)

    loads = [
        pltpu.make_async_copy(src, dst, local.at[n])
        for n, (src, dst) in enumerate([(order_hbm, order_ref), (k_hbm, k_ref), (v_hbm, v_ref), (q_hbm, q_ref)])
    ]
    for copy in loads:
        copy.start()
    w_cols = w_own.shape[1]
    w_half = pl.multiple_of(h * w_cols, 128)
    w_copy = pltpu.make_async_copy(w_ref.at[:, pl.ds(w_half, w_cols)], w_own, local.at[4])
    w_copy.start()

    def cols(group):
        if isinstance(group, int):
            return pl.ds(group * COLS, COLS)
        return pl.ds(pl.multiple_of(group * COLS, COLS), COLS)

    sub = iota((HD, COLS), 0)
    col = iota((1, COLS), 1)
    token = col % TOK
    block = token // SPAN
    step_row = token % SPAN + 8

    @pl.loop(0, GROUPS)
    def _(g):
        far_y = jnp.logical_or(g // 2 == 1, g // 2 == 2)
        hit = sub == block + 2 * (g % 2) + jnp.where(far_y, 4, 0)
        same = jnp.logical_or(g == 0, g == GROUPS - 2)
        hit = jnp.logical_or(hit, jnp.logical_and(sub == step_row, block == jnp.where(same, h, -1)))
        qt[HD : 2 * HD, cols(g)] = jnp.where(hit, 1.0, 0.0).astype(BF16)

    for k in range(CHUNKS):
        vt[k, HD:VROWS, :] = jnp.ones((VROWS - HD, KEYS), BF16)

    @pl.loop(0, TILES)
    def _(t):
        at = pl.ds(pl.multiple_of(t * TILE, TILE), TILE)
        acc[:, at] = jnp.zeros((VROWS, TILE), F32)
        mx[:, at] = jnp.full((8, TILE), -BIG, F32)

    for copy in loads:
        copy.wait()
    stacked = jnp.concatenate([q_ref[:, i * HD : (i + 1) * HD] for i in range(HEADS)], axis=0)
    qt[0:HD, cols(0)] = stacked.T
    first, second = order_ref[0].astype(F32), order_ref[1].astype(F32)
    mine = jnp.where(h == 0, first, second)
    row0 = pl.multiple_of(h * SPAN, 16)
    for stage, size, start in ((stage_a, SPLIT[0], 0), (stage_b, SPLIT[1], SPLIT[0])):
        rows = pl.ds(pl.multiple_of(row0 + start, 16), size)
        stage[0, 0:size] = k_ref[rows, :]
        stage[0, size : 2 * size] = v_ref[rows, :]
        stage[0, 2 * size :] = jnp.full((16, HD), mine, F32).astype(BF16)
    pos_tx[...] = jnp.where(iota((16, HD), 1) % 2 == 0, first, second).astype(BF16)

    pl.semaphore_wait(barrier, len(peers))

    one_a = [remote(stage_a.at[0], stage_a.at[d], one_s.at[0, d], one_r.at[0, d], device(dx=d)) for d in (1, 2, 3)]
    one_b = [remote(stage_b.at[0], stage_b.at[d], one_s.at[1, d], one_r.at[1, d], device(dz=d)) for d in range(1, 8)]
    places = [
        remote(pos_tx, pos_rx.at[n], pos_s.at[n], pos_r.at[n], where)
        for n, where in enumerate([device(dc=1), device(dy=beside), device(dy=beside, dc=1)])
    ]
    q_core = remote(qt.at[0:HD, cols(0)], qt.at[0:HD, cols(1)], q_s.at[0], q_r.at[0], device(dc=1))
    q_far, q_got, q_on = [None], [None], [None]
    for j in (1, 2, 3):
        to = lands[j]
        q_far.append(remote(qt.at[0:HD, cols(0)], qt.at[0:HD, cols(2 * to)], q_s.at[j], q_r.at[to], device(dy=shift[j])))
        q_got.append(remote(qt.at[0:HD, cols(0)], qt.at[0:HD, cols(2 * j)], q_s.at[j], q_r.at[j], device(dy=shift[j])))
        q_on.append(
            remote(qt.at[0:HD, cols(2 * j)], qt.at[0:HD, cols(2 * j + 1)], q_s.at[3 + j], q_r.at[3 + j], device(dc=1))
        )
    for copy in one_a + one_b + places + [q_core] + q_far[1:3]:
        copy.start()

    o_half = pl.multiple_of((1 - h) * w_cols, 128)
    w_rows = HD // 2

    def w_part(d, c):
        return w_oth.at[(x + d) % 4, pl.ds(pl.multiple_of(c * w_rows, w_rows), w_rows)]

    w_from = w_ref.at[pl.ds(pl.multiple_of(x * HD + core * w_rows, w_rows), w_rows), pl.ds(o_half, w_cols)]
    w_cross = remote(w_from, w_part(0, core), w_s.at[0], w_r.at[0], device(dy=across))
    w_x = [remote(w_part(0, core), w_part(0, core), w_s.at[d], w_r.at[d], device(dx=d)) for d in (1, 2, 3)]
    w_x_got = [remote(w_part(0, core), w_part(4 - d, core), w_s.at[d], w_r.at[d], device(dx=d)) for d in (1, 2, 3)]
    w_on = [remote(w_part(d, core), w_part(d, core), w_s.at[4 + d], w_r.at[4 + d], device(dc=1)) for d in range(4)]
    w_on_got = [
        remote(w_part(d, core), w_part(d, 1 - core), w_s.at[4 + d], w_r.at[4 + d], device(dc=1)) for d in range(4)
    ]

    right, left, up, down = device(dz=1), device(dz=7), device(dx=1), device(dx=3)
    whole, front, back = pl.ds(0, BUNDLE), pl.ds(0, UNIT), pl.ds(UNIT, BUNDLE - UNIT)
    hops = [
        (bundle_a, 0, 1, whole, right), (bundle_a, 0, 2, whole, left), (bundle_b, 0, 1, whole, up), (bundle_b, 0, 2, whole, down),
        (bundle_a, 1, 3, whole, right), (bundle_a, 2, 4, whole, left), (bundle_b, 1, 3, front, up), (bundle_b, 2, 3, back, down),
        (bundle_a, 3, 5, whole, right), (bundle_a, 4, 6, whole, left),
        (bundle_a, 5, 7, front, right), (bundle_a, 6, 7, back, left),
    ]
    ring = [
        remote(bundle.at[src, part], bundle.at[dst, part], ring_s.at[n], ring_r.at[n], where)
        for n, (bundle, src, dst, part, where) in enumerate(hops)
    ]

    def assemble(bundle, stage, blocks, size):
        row = iota((16, HD), 0)
        tile = jnp.zeros((16, HD), F32)
        for j in range(blocks):
            bundle[0, j * size : (j + 1) * size] = stage[j, 0:size]
            bundle[0, UNIT + j * size : UNIT + (j + 1) * size] = stage[j, size : 2 * size]
            tile = jnp.where(row == j, stage[j, 2 * size :].astype(F32), tile)
        bundle[0, 2 * UNIT :] = tile.astype(BF16)

    def prepare(k):
        pair = iota((16, HD), 1) // 2
        limit = jnp.full((16, HD), 1e6, F32)
        for n, tile in enumerate([pos_tx[...], pos_rx[0], pos_rx[1], pos_rx[2]]):
            limit = jnp.where(pair == n, tile.astype(F32), limit)
        limit = limit[0:1]
        for n, (bundle, at, route) in enumerate([(bundle_a, 2 * k, 0), (bundle_a, 2 * k + 1, 0), (bundle_b, k, 1)]):
            base, size = n * UNIT, SPLIT[route]
            kaug[k, base : base + UNIT, 0:HD] = bundle[at, 0:UNIT]
            vt[k, 0:HD, base : base + UNIT] = bundle[at, UNIT : 2 * UNIT].T
            tile = bundle[at, 2 * UNIT :].astype(F32)
            for j in range(BLOCKS[route]):
                bias = jnp.broadcast_to(jnp.where(tile[j : j + 1] <= limit, 0.0, -BIG), (size, HD))
                if isinstance(k, int) and k == 0 and j == 0 and n != 1:
                    key = iota((size, HD), 0) + (SPLIT[0] if route else 0)
                    tok = iota((size, HD), 1) - 8
                    late = jnp.logical_and(jnp.logical_and(tok >= 0, tok < SPAN), key > tok)
                    bias = jnp.where(late, -BIG, bias)
                kaug[k, base + j * size : base + (j + 1) * size, HD:] = bias.astype(BF16)

    def tile_at(t):
        return pl.ds(t * TILE, TILE) if isinstance(t, int) else pl.ds(pl.multiple_of(t * TILE, TILE), TILE)

    def scores(k, t, slot):
        s = jnp.dot(kaug[k], qt[:, tile_at(t)], preferred_element_type=F32)
        sbuf[slot] = s
        return jnp.max(s, axis=0, keepdims=True)

    def step(now, following, slot, top):
        k, t = now
        at = tile_at(t)
        old = mx[:, at]
        new = jnp.maximum(old, top)
        fade = jnp.exp2((old - new) * SCALE)
        mx[:, at] = new
        if following is not None:
            top = scores(*following, 1 - slot)
        p = jnp.exp2((sbuf[slot] - new[:1]) * SCALE).astype(BF16)
        acc[:, at] = acc[:, at] * fade[:1] + jnp.dot(vt[k], p, preferred_element_type=F32)
        return top

    def receive(*copies):
        for copy in copies:
            copy.wait_recv()

    def start(*copies):
        for copy in copies:
            copy.start()

    def stats(group):
        return jnp.where(iota((8, COLS), 0) < 4, mx[:, cols(group)], acc[HD : HD + 8, cols(group)])

    def merge(group, part, stat):
        there, here = stat[0:1], mx[0:1, cols(group)]
        top = jnp.maximum(there, here)
        ours, theirs = jnp.exp2((here - top) * SCALE), jnp.exp2((there - top) * SCALE)
        acc[0:HD, cols(group)] = acc[0:HD, cols(group)] * ours + part.astype(F32) * theirs
        total = acc[HD : HD + 8, cols(group)] * ours + stat[4:5] * theirs
        acc[HD : HD + 8, cols(group)] = total
        mx[:, cols(group)] = jnp.broadcast_to(top, (8, COLS))

    def part_copies(j):
        return (
            remote(p1_tx.at[j], p1_rx.at[j], d_s.at[0, j], d_r.at[0, j], device(dc=1)),
            remote(s1_tx.at[j], s1_rx.at[j], d_s.at[1, j], d_r.at[1, j], device(dc=1)),
        )

    def sum_copies(j, to, where):
        return (
            remote(p2_tx.at[j], p2_rx.at[to], e_s.at[0, j], e_r.at[0, to], where),
            remote(s2_tx.at[j], s2_rx.at[to], e_s.at[1, j], e_r.at[1, to], where),
        )

    c_copy = remote(c_tx, c_rx, tail_sem.at[0], tail_sem.at[1], device(dy=2))

    def hand_over(j):
        p1_tx[j] = acc[0:HD, cols(2 * j + 1)].astype(BF16)
        s1_tx[j] = stats(2 * j + 1)
        start(*part_copies(j))

    def send_sum(j):
        receive(*part_copies(j))
        merge(2 * j, p1_rx[j], s1_rx[j])
        p2_tx[j] = acc[0:HD, cols(2 * j)].astype(BF16)
        s2_tx[j] = stats(2 * j)
        turn = j + (j // 2) * (5 - 2 * j)
        to = 3 * (j // 3) + (1 - j // 3) * (3 - j)
        start(*sum_copies(j, to, device(dy=turn)))

    receive(*one_a)
    start(q_far[3])
    assemble(bundle_a, stage_a, BLOCKS[0], SPLIT[0])
    start(ring[0], ring[1])
    receive(*one_b)
    assemble(bundle_b, stage_b, BLOCKS[1], SPLIT[1])
    start(ring[2], ring[3])
    receive(*places)
    receive(ring[0], ring[1])
    start(ring[4], ring[5])
    receive(q_got[1])
    start(q_on[1])
    prepare(0)
    top = scores(0, 0, 0)

    for t in range(TILES):
        if t == 0:
            receive(q_core, q_got[2])
            start(q_on[2])
        if t == 2:
            receive(q_on[1])
        if t == 3:
            start(w_cross)
        if t == 5:
            receive(q_on[2], q_got[3])
            start(q_on[3])
        if t == 9:
            receive(q_on[3], ring[2], ring[3], ring[4], ring[5])
            start(ring[6], ring[7], ring[8], ring[9])
        if t == TILES - 1:
            prepare(1)
        top = step((0, t), (0, t + 1) if t < TILES - 1 else (1, 0), t % 2, top)

    def second(i, top):
        base = i * 6
        for t in range(6):
            if t == 1:
                @pl.when(i == 1)
                def _():
                    receive(ring[8], ring[9])
                    start(ring[10], ring[11])
            if t == 5:
                @pl.when(i == 1)
                def _():
                    prepare(2)
                    receive(w_cross)
                    start(*w_x, w_on[0])
                following = (jnp.where(i == 1, 2, 1), jnp.where(i == 1, TILES - 1, 6))
            else:
                following = (1, base + t + 1)
            top = step((1, base + t), following, t % 2, top)
        return top

    top = lax.fori_loop(0, 2, second, top)
    receive(ring[6], ring[7], ring[10], ring[11])
    prepare(3)

    def far(i, top):
        j = 3 - i
        base = 3 * j
        for n in range(6):
            k, t = 2 + n % 2, base + 2 - n // 2
            if n == 2:
                pl.when(i > 0)(lambda: send_sum(j + 1))
            if n == 4:
                hand_over(j)
            following = (2 + (n + 1) % 2, base + 2 - (n + 1) // 2) if n < 5 else (2, base - 1)
            top = step((k, t), following, n % 2, top)
        return top

    top = lax.fori_loop(0, 3, far, top)
    for n in range(6):
        k, t = 2 + n % 2, 2 - n // 2
        if n == 2:
            send_sum(1)
        if n == 4:
            hand_over(0)
        top = step((k, t), (2 + (n + 1) % 2, 2 - (n + 1) // 2) if n < 5 else None, n % 2, top)

    receive(*part_copies(0))
    merge(0, p1_rx[0], s1_rx[0])
    for j in (3, 2, 1):
        receive(*sum_copies(j, j, device(dy=1)))
        merge(0, p2_rx[j], s2_rx[j])
    c_tx[...] = (acc[0:HD, cols(0)] / acc[HD : HD + 1, cols(0)]).astype(BF16)
    c_copy.start()
    receive(*w_x_got)
    start(*w_on[1:])
    w_copy.wait()

    def context(ref):
        flat = ref[...].T
        return jnp.concatenate([flat[i * TOK : (i + 1) * TOK] for i in range(HEADS)], axis=1)

    own = context(c_tx)

    @pl.loop(0, w_cols // TILE)
    def _(n):
        at = pl.ds(pl.multiple_of(n * TILE, TILE), TILE)
        pacc[:, at] = jnp.dot(own, w_own[:, at], preferred_element_type=F32)

    receive(c_copy, *w_on_got)
    other = context(c_rx)

    @pl.loop(0, w_cols // TILE)
    def _(n):
        at = pl.ds(pl.multiple_of(n * TILE, TILE), TILE)
        term = jnp.dot(other, w_oth[:, :, at].reshape(HEADS * HD, TILE), preferred_element_type=F32)
        o_ref[:, at] = (pacc[:, at] + term).astype(BF16)

    sent = one_a + one_b + places + [q_core] + q_far[1:] + q_on[1:] + ring + [w_cross] + w_x + w_on + [c_copy]
    for j in range(4):
        sent += part_copies(j)
    for j in (1, 2, 3):
        sent += sum_copies(j, lands[j], device(dy=shift[j]))
    for copy in sent:
        copy.wait_send()


def body(queries, keys, values, span_order, w_out):
    width = w_out.shape[1] // 2
    vmem = pl.BlockSpec(memory_space=pltpu.VMEM)
    dma = pltpu.SemaphoreType.DMA
    scratch = [
        pltpu.VMEM((TOK, HEADS * HD), BF16),
        pltpu.VMEM((TOK, HD), BF16),
        pltpu.VMEM((TOK, HD), BF16),
        pltpu.SMEM((2,), jnp.int32),
        pltpu.VMEM((2 * HD, GROUPS * COLS), BF16),
        pltpu.VMEM((16, HD), BF16),
        pltpu.VMEM((3, 16, HD), BF16),
        pltpu.VMEM((4, 2 * SPLIT[0] + 16, HD), BF16),
        pltpu.VMEM((8, 2 * SPLIT[1] + 16, HD), BF16),
        pltpu.VMEM((8, BUNDLE, HD), BF16),
        pltpu.VMEM((4, BUNDLE, HD), BF16),
        pltpu.VMEM((CHUNKS, KEYS, 2 * HD), BF16),
        pltpu.VMEM((CHUNKS, VROWS, KEYS), BF16),
        pltpu.VMEM((2, KEYS, TILE), F32),
        pltpu.VMEM((VROWS, GROUPS * COLS), F32),
        pltpu.VMEM((8, GROUPS * COLS), F32),
        pltpu.VMEM((HEADS * HD, width), BF16),
        pltpu.VMEM((HEADS, HD, width), BF16),
        pltpu.VMEM((TOK, width), F32),
        pltpu.VMEM((4, HD, COLS), BF16),
        pltpu.VMEM((4, HD, COLS), BF16),
        pltpu.VMEM((4, 8, COLS), F32),
        pltpu.VMEM((4, 8, COLS), F32),
        pltpu.VMEM((4, HD, COLS), BF16),
        pltpu.VMEM((4, HD, COLS), BF16),
        pltpu.VMEM((4, 8, COLS), F32),
        pltpu.VMEM((4, 8, COLS), F32),
        pltpu.VMEM((HD, COLS), BF16),
        pltpu.VMEM((HD, COLS), BF16),
        dma((2, 8)), dma((2, 8)), dma((7,)), dma((7,)), dma((3,)), dma((3,)), dma((12,)), dma((12,)), dma((8,)), dma((8,)),
        dma((5,)), dma((2, 4)), dma((2, 4)), dma((2, 4)), dma((2, 4)), dma((2,)),
    ]
    return pl.pallas_call(
        kernel,
        out_shape=jax.ShapeDtypeStruct((TOK, width), BF16),
        in_specs=[pl.BlockSpec(memory_space=pl.ANY)] * 5,
        out_specs=vmem,
        scratch_shapes=scratch,
        compiler_params=pltpu.CompilerParams(
            collective_id=0, has_side_effects=True, vmem_limit_bytes=56 * 2**20
        ),
    )(queries, keys, values, span_order, w_out)


def solution(mesh):
    return jax.shard_map(
        body,
        mesh=mesh,
        in_specs=(P("ctx", "grp"), P("ctx", None), P("ctx", None), P("ctx"), P("grp", None)),
        out_specs=P("ctx", "grp"),
        check_vma=False,
    )
```

```python
import functools

import jax
import jax.numpy as jnp
from jax import lax
from jax.experimental import pallas as pl
from jax.experimental.pallas import tpu as pltpu
from jax.sharding import PartitionSpec as P

HD = 128
HEADS = 4
TOK = 192
SPAN = 96
SPLIT = (64, 32)
BLOCKS = (4, 8)
COLS = HEADS * TOK
UNIT = 256
TILE = 512
GROUPS = 8
TILES = GROUPS * COLS // TILE
KEYS = 3 * UNIT
CHUNKS = 4
BUNDLE = 2 * UNIT + 16
VROWS = 144
MESH = pl.DeviceIdType.MESH
BIG = 2.0**100
SCALE = HD**-0.5 * 1.4426950408889634
F32 = jnp.float32
BF16 = jnp.bfloat16


def iota(shape, dim):
    return lax.broadcasted_iota(jnp.int32, shape, dim)


def kernel(
    q_hbm, k_hbm, v_hbm, order_hbm, w_ref, o_ref,
    q_ref, k_ref, v_ref, order_ref,
    qt, pos_tx, pos_rx, stage_a, stage_b, bundle_a, bundle_b, kaug, vt, sbuf, acc, mx, w_own, w_oth, pacc,
    p1_tx, p1_rx, s1_tx, s1_rx, p2_tx, p2_rx, s2_tx, s2_rx, c_tx, c_rx,
    one_s, one_r, q_s, q_r, pos_s, pos_r, ring_s, ring_r, w_s, w_r, local, d_s, d_r, e_s, e_r, tail_sem,
):
    ctx, h = lax.axis_index("ctx"), lax.axis_index("grp")
    z, ylo, x, core = ctx // 16, (ctx // 8) % 2, (ctx // 2) % 4, ctx % 2
    y = 2 * h + ylo

    def device(dz=0, dy=0, dx=0, dc=0):
        z1, x1, y1 = (z + dz) % 8, (x + dx) % 4, (y + dy) % 4
        c1 = 1 - core if dc else core
        return (((z1 * 2 + y1 % 2) * 4 + x1) * 2 + c1, y1 // 2)

    beside = 1 - 2 * ylo + 4
    across = 3 - 2 * y + 4

    def remote(src, dst, send, recv, where):
        return pltpu.make_async_remote_copy(
            src_ref=src, dst_ref=dst, send_sem=send, recv_sem=recv, device_id=where, device_id_type=MESH
        )

    shift, lands = (0, 1, 3, 2), (0, 2, 1, 3)
    peers = [device(dx=d) for d in (1, 2, 3)] + [device(dz=d) for d in range(1, 8)]
    peers += [device(dy=d) for d in (1, 2, 3)] + [device(dc=1), device(dy=beside, dc=1)]
    barrier = pltpu.get_barrier_semaphore()
    for peer in peers:
        pl.semaphore_signal(barrier, inc=1, device_id=peer, device_id_type=MESH)

    loads = [
        pltpu.make_async_copy(src, dst, local.at[n])
        for n, (src, dst) in enumerate([(order_hbm, order_ref), (k_hbm, k_ref), (v_hbm, v_ref), (q_hbm, q_ref)])
    ]
    for copy in loads:
        copy.start()
    w_cols = w_own.shape[1]
    w_half = pl.multiple_of(h * w_cols, 128)
    w_copy = pltpu.make_async_copy(w_ref.at[:, pl.ds(w_half, w_cols)], w_own, local.at[4])
    w_copy.start()

    def cols(group):
        if isinstance(group, int):
            return pl.ds(group * COLS, COLS)
        return pl.ds(pl.multiple_of(group * COLS, COLS), COLS)

    for copy in loads[:3]:
        copy.wait()
    first, second = order_ref[0].astype(F32), order_ref[1].astype(F32)
    mine = jnp.where(h == 0, first, second)
    row0 = pl.multiple_of(h * SPAN, 16)
    for stage, size, start in ((stage_a, SPLIT[0], 0), (stage_b, SPLIT[1], SPLIT[0])):
        rows = pl.ds(pl.multiple_of(row0 + start, 16), size)
        stage[0, 0:size] = k_ref[rows, :]
        stage[0, size : 2 * size] = v_ref[rows, :]
        stage[0, 2 * size :] = jnp.full((16, HD), mine, F32).astype(BF16)
    pos_tx[...] = jnp.where(iota((16, HD), 1) % 2 == 0, first, second).astype(BF16)

    pl.semaphore_wait(barrier, len(peers))

    one_a = [remote(stage_a.at[0], stage_a.at[d], one_s.at[0, d], one_r.at[0, d], device(dx=d)) for d in (1, 2, 3)]
    one_b = [remote(stage_b.at[0], stage_b.at[d], one_s.at[1, d], one_r.at[1, d], device(dz=d)) for d in range(1, 8)]
    places = [
        remote(pos_tx, pos_rx.at[n], pos_s.at[n], pos_r.at[n], where)
        for n, where in enumerate([device(dc=1), device(dy=beside), device(dy=beside, dc=1)])
    ]
    q_core = remote(qt.at[0:HD, cols(0)], qt.at[0:HD, cols(1)], q_s.at[0], q_r.at[0], device(dc=1))
    q_far, q_got, q_on = [None], [None], [None]
    for j in (1, 2, 3):
        to = lands[j]
        q_far.append(remote(qt.at[0:HD, cols(0)], qt.at[0:HD, cols(2 * to)], q_s.at[j], q_r.at[to], device(dy=shift[j])))
        q_got.append(remote(qt.at[0:HD, cols(0)], qt.at[0:HD, cols(2 * j)], q_s.at[j], q_r.at[j], device(dy=shift[j])))
        q_on.append(
            remote(qt.at[0:HD, cols(2 * j)], qt.at[0:HD, cols(2 * j + 1)], q_s.at[3 + j], q_r.at[3 + j], device(dc=1))
        )
    for copy in one_a + one_b + places:
        copy.start()
    loads[3].wait()
    stacked = jnp.concatenate([q_ref[:, i * HD : (i + 1) * HD] for i in range(HEADS)], axis=0)
    qt[0:HD, cols(0)] = stacked.T
    for copy in [q_core] + q_far[1:3]:
        copy.start()

    o_half = pl.multiple_of((1 - h) * w_cols, 128)
    w_rows = HD // 2

    def w_part(d, c):
        return w_oth.at[(x + d) % 4, pl.ds(pl.multiple_of(c * w_rows, w_rows), w_rows)]

    w_from = w_ref.at[pl.ds(pl.multiple_of(x * HD + core * w_rows, w_rows), w_rows), pl.ds(o_half, w_cols)]
    w_cross = remote(w_from, w_part(0, core), w_s.at[0], w_r.at[0], device(dy=across))
    w_x = [remote(w_part(0, core), w_part(0, core), w_s.at[d], w_r.at[d], device(dx=d)) for d in (1, 2, 3)]
    w_x_got = [remote(w_part(0, core), w_part(4 - d, core), w_s.at[d], w_r.at[d], device(dx=d)) for d in (1, 2, 3)]
    w_on = [remote(w_part(d, core), w_part(d, core), w_s.at[4 + d], w_r.at[4 + d], device(dc=1)) for d in range(4)]
    w_on_got = [
        remote(w_part(d, core), w_part(d, 1 - core), w_s.at[4 + d], w_r.at[4 + d], device(dc=1)) for d in range(4)
    ]

    right, left, up, down = device(dz=1), device(dz=7), device(dx=1), device(dx=3)
    whole, front, back = pl.ds(0, BUNDLE), pl.ds(0, UNIT), pl.ds(UNIT, BUNDLE - UNIT)
    hops = [
        (bundle_a, 0, 1, whole, right), (bundle_a, 0, 2, whole, left), (bundle_b, 0, 1, whole, up), (bundle_b, 0, 2, whole, down),
        (bundle_a, 1, 3, whole, right), (bundle_a, 2, 4, whole, left), (bundle_b, 1, 3, front, up), (bundle_b, 2, 3, back, down),
        (bundle_a, 3, 5, whole, right), (bundle_a, 4, 6, whole, left),
        (bundle_a, 5, 7, front, right), (bundle_a, 6, 7, back, left),
    ]
    ring = [
        remote(bundle.at[src, part], bundle.at[dst, part], ring_s.at[n], ring_r.at[n], where)
        for n, (bundle, src, dst, part, where) in enumerate(hops)
    ]

    def assemble(bundle, stage, blocks, size):
        row = iota((16, HD), 0)
        tile = jnp.zeros((16, HD), F32)
        for j in range(blocks):
            bundle[0, j * size : (j + 1) * size] = stage[j, 0:size]
            bundle[0, UNIT + j * size : UNIT + (j + 1) * size] = stage[j, size : 2 * size]
            tile = jnp.where(row == j, stage[j, 2 * size :].astype(F32), tile)
        bundle[0, 2 * UNIT :] = tile.astype(BF16)

    def prepare(k):
        pair = iota((16, HD), 1) // 2
        limit = jnp.full((16, HD), 1e6, F32)
        for n, tile in enumerate([pos_tx[...], pos_rx[0], pos_rx[1], pos_rx[2]]):
            limit = jnp.where(pair == n, tile.astype(F32), limit)
        limit = limit[0:1]
        for n, (bundle, at, route) in enumerate([(bundle_a, 2 * k, 0), (bundle_a, 2 * k + 1, 0), (bundle_b, k, 1)]):
            base, size = n * UNIT, SPLIT[route]
            kaug[k, base : base + UNIT, 0:HD] = bundle[at, 0:UNIT]
            vt[k, 0:HD, base : base + UNIT] = bundle[at, UNIT : 2 * UNIT].T
            tile = bundle[at, 2 * UNIT :].astype(F32)
            for j in range(BLOCKS[route]):
                bias = jnp.broadcast_to(jnp.where(tile[j : j + 1] <= limit, 0.0, -BIG), (size, HD))
                if isinstance(k, int) and k == 0 and j == 0 and n != 1:
                    key = iota((size, HD), 0) + (SPLIT[0] if route else 0)
                    tok = iota((size, HD), 1) - 8
                    late = jnp.logical_and(jnp.logical_and(tok >= 0, tok < SPAN), key > tok)
                    bias = jnp.where(late, -BIG, bias)
                kaug[k, base + j * size : base + (j + 1) * size, HD:] = bias.astype(BF16)

    def tile_at(t):
        return pl.ds(t * TILE, TILE) if isinstance(t, int) else pl.ds(pl.multiple_of(t * TILE, TILE), TILE)

    def scores(k, t, slot):
        s = jnp.dot(kaug[k], qt[:, tile_at(t)], preferred_element_type=F32)
        sbuf[slot] = s
        return jnp.max(s, axis=0, keepdims=True)

    def step(now, following, slot, top):
        k, t = now
        at = tile_at(t)
        old = mx[:, at]
        new = jnp.maximum(old, top)
        fade = jnp.exp2((old - new) * SCALE)
        mx[:, at] = new
        if following is not None:
            top = scores(*following, 1 - slot)
        p = jnp.exp2((sbuf[slot] - new[:1]) * SCALE).astype(BF16)
        acc[:, at] = acc[:, at] * fade[:1] + jnp.dot(vt[k], p, preferred_element_type=F32)
        return top

    def receive(*copies):
        for copy in copies:
            copy.wait_recv()

    def start(*copies):
        for copy in copies:
            copy.start()

    def stats(group):
        return jnp.where(iota((8, COLS), 0) < 4, mx[:, cols(group)], acc[HD : HD + 8, cols(group)])

    def merge(group, part, stat):
        there, here = stat[0:1], mx[0:1, cols(group)]
        top = jnp.maximum(there, here)
        ours, theirs = jnp.exp2((here - top) * SCALE), jnp.exp2((there - top) * SCALE)
        acc[0:HD, cols(group)] = acc[0:HD, cols(group)] * ours + part.astype(F32) * theirs
        total = acc[HD : HD + 8, cols(group)] * ours + stat[4:5] * theirs
        acc[HD : HD + 8, cols(group)] = total
        mx[:, cols(group)] = jnp.broadcast_to(top, (8, COLS))

    def part_copies(j):
        return (
            remote(p1_tx.at[j], p1_rx.at[j], d_s.at[0, j], d_r.at[0, j], device(dc=1)),
            remote(s1_tx.at[j], s1_rx.at[j], d_s.at[1, j], d_r.at[1, j], device(dc=1)),
        )

    def sum_copies(j, to, where):
        return (
            remote(p2_tx.at[j], p2_rx.at[to], e_s.at[0, j], e_r.at[0, to], where),
            remote(s2_tx.at[j], s2_rx.at[to], e_s.at[1, j], e_r.at[1, to], where),
        )

    c_copy = remote(c_tx, c_rx, tail_sem.at[0], tail_sem.at[1], device(dy=2))

    def hand_over(j):
        p1_tx[j] = acc[0:HD, cols(2 * j + 1)].astype(BF16)
        s1_tx[j] = stats(2 * j + 1)
        start(*part_copies(j))

    def send_sum(j):
        receive(*part_copies(j))
        merge(2 * j, p1_rx[j], s1_rx[j])
        p2_tx[j] = acc[0:HD, cols(2 * j)].astype(BF16)
        s2_tx[j] = stats(2 * j)
        turn = j + (j // 2) * (5 - 2 * j)
        to = 3 * (j // 3) + (1 - j // 3) * (3 - j)
        start(*sum_copies(j, to, device(dy=turn)))

    sub = iota((HD, COLS), 0)
    col = iota((1, COLS), 1)
    token = col % TOK
    block = token // SPAN
    step_row = token % SPAN + 8

    @pl.loop(0, GROUPS)
    def _(g):
        far_y = jnp.logical_or(g // 2 == 1, g // 2 == 2)
        hit = sub == block + 2 * (g % 2) + jnp.where(far_y, 4, 0)
        same = jnp.logical_or(g == 0, g == GROUPS - 2)
        hit = jnp.logical_or(hit, jnp.logical_and(sub == step_row, block == jnp.where(same, h, -1)))
        qt[HD : 2 * HD, cols(g)] = jnp.where(hit, 1.0, 0.0).astype(BF16)

    for k in range(CHUNKS):
        vt[k, HD:VROWS, :] = jnp.ones((VROWS - HD, KEYS), BF16)

    @pl.loop(0, TILES)
    def _(t):
        at = pl.ds(pl.multiple_of(t * TILE, TILE), TILE)
        acc[:, at] = jnp.zeros((VROWS, TILE), F32)
        mx[:, at] = jnp.full((8, TILE), -BIG, F32)

    receive(*one_a)
    start(q_far[3])
    assemble(bundle_a, stage_a, BLOCKS[0], SPLIT[0])
    start(ring[0], ring[1])
    receive(*one_b)
    assemble(bundle_b, stage_b, BLOCKS[1], SPLIT[1])
    start(ring[2], ring[3])
    receive(*places)
    receive(ring[0], ring[1])
    start(ring[4], ring[5])
    receive(q_got[1])
    start(q_on[1])
    prepare(0)
    top = scores(0, 0, 0)

    for t in range(TILES):
        if t == 0:
            receive(q_core, q_got[2])
            start(q_on[2])
        if t == 2:
            receive(q_on[1])
        if t == 3:
            start(w_cross)
        if t == 5:
            receive(q_on[2], q_got[3])
            start(q_on[3])
        if t == 7:
            receive(q_on[3], ring[2], ring[3], ring[4], ring[5])
            start(ring[6], ring[7], ring[8], ring[9])
        if t == TILES - 1:
            prepare(1)
        top = step((0, t), (0, t + 1) if t < TILES - 1 else (1, 3), t % 2, top)

    for n, t in enumerate(range(3, TILES)):
        if n == 7:
            receive(w_cross)
            start(*w_x, w_on[0])
        if n == 4:
            receive(ring[8], ring[9])
            start(ring[10], ring[11])
        if n == 8:
            prepare(2)
        top = step((1, t), (1, t + 1) if n < 8 else (2, TILES - 1), n % 2, top)
    receive(ring[6], ring[7], ring[10], ring[11])
    prepare(3)

    def far(i, top):
        j = 3 - i
        base = 3 * j
        for n in range(6):
            k, t = 2 + n % 2, base + 2 - n // 2
            if n == 2:
                pl.when(i > 0)(lambda: send_sum(j + 1))
            if n == 4:
                hand_over(j)
            following = (2 + (n + 1) % 2, base + 2 - (n + 1) // 2) if n < 5 else (jnp.where(i == 2, 1, 2), base - 1)
            top = step((k, t), following, (n + 1) % 2, top)
        return top

    top = lax.fori_loop(0, 3, far, top)
    last = [(k, t) for t in (2, 1, 0) for k in (1, 2, 3)]
    for n, now in enumerate(last):
        if n == 2:
            send_sum(1)
        if n == 6:
            hand_over(0)
        if n == 7:
            receive(*sum_copies(3, 3, device(dy=1)))
            merge(0, p2_rx[3], s2_rx[3])
        top = step(now, last[n + 1] if n < 8 else None, (n + 1) % 2, top)

    receive(*part_copies(0))
    merge(0, p1_rx[0], s1_rx[0])
    for j in (2, 1):
        receive(*sum_copies(j, j, device(dy=1)))
        merge(0, p2_rx[j], s2_rx[j])
    c_tx[...] = (acc[0:HD, cols(0)] / acc[HD : HD + 1, cols(0)]).astype(BF16)
    c_copy.start()
    receive(*w_x_got)
    start(*w_on[1:])
    w_copy.wait()

    def context(ref):
        flat = ref[...].T
        return jnp.concatenate([flat[i * TOK : (i + 1) * TOK] for i in range(HEADS)], axis=1)

    own = context(c_tx)

    @pl.loop(0, w_cols // TILE)
    def _(n):
        at = pl.ds(pl.multiple_of(n * TILE, TILE), TILE)
        pacc[:, at] = jnp.dot(own, w_own[:, at], preferred_element_type=F32)

    receive(c_copy, *w_on_got)
    other = context(c_rx)

    @pl.loop(0, w_cols // TILE)
    def _(n):
        at = pl.ds(pl.multiple_of(n * TILE, TILE), TILE)
        term = jnp.dot(other, w_oth[:, :, at].reshape(HEADS * HD, TILE), preferred_element_type=F32)
        o_ref[:, at] = (pacc[:, at] + term).astype(BF16)

    sent = one_a + one_b + places + [q_core] + q_far[1:] + q_on[1:] + ring + [w_cross] + w_x + w_on + [c_copy]
    for j in range(4):
        sent += part_copies(j)
    for j in (1, 2, 3):
        sent += sum_copies(j, lands[j], device(dy=shift[j]))
    for copy in sent:
        copy.wait_send()


def body(queries, keys, values, span_order, w_out):
    width = w_out.shape[1] // 2
    vmem = pl.BlockSpec(memory_space=pltpu.VMEM)
    dma = pltpu.SemaphoreType.DMA
    scratch = [
        pltpu.VMEM((TOK, HEADS * HD), BF16),
        pltpu.VMEM((TOK, HD), BF16),
        pltpu.VMEM((TOK, HD), BF16),
        pltpu.SMEM((2,), jnp.int32),
        pltpu.VMEM((2 * HD, GROUPS * COLS), BF16),
        pltpu.VMEM((16, HD), BF16),
        pltpu.VMEM((3, 16, HD), BF16),
        pltpu.VMEM((4, 2 * SPLIT[0] + 16, HD), BF16),
        pltpu.VMEM((8, 2 * SPLIT[1] + 16, HD), BF16),
        pltpu.VMEM((8, BUNDLE, HD), BF16),
        pltpu.VMEM((4, BUNDLE, HD), BF16),
        pltpu.VMEM((CHUNKS, KEYS, 2 * HD), BF16),
        pltpu.VMEM((CHUNKS, VROWS, KEYS), BF16),
        pltpu.VMEM((2, KEYS, TILE), F32),
        pltpu.VMEM((VROWS, GROUPS * COLS), F32),
        pltpu.VMEM((8, GROUPS * COLS), F32),
        pltpu.VMEM((HEADS * HD, width), BF16),
        pltpu.VMEM((HEADS, HD, width), BF16),
        pltpu.VMEM((TOK, width), F32),
        pltpu.VMEM((4, HD, COLS), BF16),
        pltpu.VMEM((4, HD, COLS), BF16),
        pltpu.VMEM((4, 8, COLS), F32),
        pltpu.VMEM((4, 8, COLS), F32),
        pltpu.VMEM((4, HD, COLS), BF16),
        pltpu.VMEM((4, HD, COLS), BF16),
        pltpu.VMEM((4, 8, COLS), F32),
        pltpu.VMEM((4, 8, COLS), F32),
        pltpu.VMEM((HD, COLS), BF16),
        pltpu.VMEM((HD, COLS), BF16),
        dma((2, 8)), dma((2, 8)), dma((7,)), dma((7,)), dma((3,)), dma((3,)), dma((12,)), dma((12,)), dma((8,)), dma((8,)),
        dma((5,)), dma((2, 4)), dma((2, 4)), dma((2, 4)), dma((2, 4)), dma((2,)),
    ]
    return pl.pallas_call(
        kernel,
        out_shape=jax.ShapeDtypeStruct((TOK, width), BF16),
        in_specs=[pl.BlockSpec(memory_space=pl.ANY)] * 5,
        out_specs=vmem,
        scratch_shapes=scratch,
        compiler_params=pltpu.CompilerParams(
            collective_id=0, has_side_effects=True, vmem_limit_bytes=56 * 2**20
        ),
    )(queries, keys, values, span_order, w_out)


def solution(mesh):
    return jax.shard_map(
        body,
        mesh=mesh,
        in_specs=(P("ctx", "grp"), P("ctx", None), P("ctx", None), P("ctx"), P("grp", None)),
        out_specs=P("ctx", "grp"),
        check_vma=False,
    )
```
